32 devices in a mesh: parts: 2 (over x), feat: 8 (over z, y), tok: 2 (over core).
Axes of the slice: x: 2, y: 2, z: 4, core: 2. Of those that a mesh axis runs over, the one named last changes fastest.
Arguments:
- token_index: int32 [16, 16], P(('parts', 'feat')), parts along dimension 0, may hold values from 0 to 15, each once within a row
- act_pool: bfloat16 [256, 14336], P(('parts', 'feat'), 'tok'), parts along dimension 0, may hold values from -6 to 6
- grad_pool: bfloat16 [256, 4096], P(('parts', 'feat'), 'tok'), parts along dimension 0, may hold values from -6 to 6
- basis_in: bfloat16 [28672, 14336], P(('parts', 'tok'), 'feat'), parts along dimension 0, may hold values from -0.046875 to 0.046875
- basis_out: bfloat16 [8192, 4096], P(('parts', 'tok'), 'feat'), parts along dimension 0, may hold values from -0.09375 to 0.09375
- precond: bfloat16 [4, 4096, 14336], P('parts', None, ('feat', 'tok')), parts along dimension 0, may hold values from -0.0007324219 to 0.0007324219
Outputs:
- scores: float32 [4, 128], P('parts'), parts along dimension 0
- act_rot: bfloat16 [256, 14336], P('parts', ('feat', 'tok')), parts along dimension 0
- grad_rot: bfloat16 [256, 4096], P('parts', ('feat', 'tok')), parts along dimension 0
The draws below stay inside these ranges and needn't reach their ends.
There are 2 independent parts, one for each index of `parts`. The reference program is written for one: setup_inputs(seed, part) draws one part's arguments, and reference() takes and returns one part's arrays. A program takes and returns all parts, laid end to end along the dimension named above; each array names one. Nothing has to cross between parts.
Inputs may be any that keep to these rules, and one draw needn't show every extreme that they name: Each row of token_index orders the 16 stored tokens of one shard, each once.
All inputs are finite; a program needn't handle non-finite values.
Results may differ from the reference program's by a relative error of at most 0.006.
Values may be sent and summed in bfloat16 or wider, within the bound.
No kernel may reach another device: no remote copies, remote signals or barrier semaphores. Data moves between devices by JAX's collectives and lax.ppermute only.
A program may use at most 128 MiB of HBM per device.

```python
import jax
import jax.numpy as jnp
from jax import lax

IN = 14336
OUT = 4096
QUERIES = 2
TOK_SHARD = 16
TOKENS = 128
N_FEAT = 8


def shard_levels(rng, dims, cuts, least, largest):
    gain, own = 1.0, jax.random.fold_in(rng, 6)
    for position, parts in cuts:
        steps = jnp.exp(jax.random.uniform(jax.random.fold_in(own, position), (parts,), jnp.float32, least / len(cuts), largest / len(cuts)))
        gain = gain * jnp.repeat(steps, dims[position] // parts).reshape([-1 if axis == position else 1 for axis in range(len(dims))])
    return gain


def gaussian(key, extent, scale, most, cuts=(), kind=jnp.bfloat16):
    array = scale * jax.random.normal(key, extent, jnp.float32)
    if cuts:
        array = array * shard_levels(key, extent, cuts, -0.22, 0.18)
    return jnp.clip(array, -most, most).astype(kind)


def setup_inputs(seed: int = 0, part: int = 0) -> dict:
    streams_of = jax.random.split(jax.random.key(seed), 7)
    own_keys = jax.random.split(jax.random.fold_in(streams_of[6], part), 7)
    return {
        "token_index": jax.vmap(lambda own: jax.random.permutation(own, TOK_SHARD))(jax.random.split(own_keys[0], N_FEAT)).reshape((N_FEAT, TOK_SHARD)).astype(jnp.int32),
        "act_pool": gaussian(own_keys[1], (TOKENS, IN), 1.0, 6.0, ((0, 8), (1, 2))),
        "grad_pool": gaussian(own_keys[2], (TOKENS, OUT), 1.0, 6.0, ((0, 8), (1, 2))),
        "basis_in": gaussian(own_keys[3], (IN, IN), IN ** -0.5, 0.046875, ((0, 2), (1, 8))),
        "basis_out": gaussian(own_keys[4], (OUT, OUT), OUT ** -0.5, 0.09375, ((0, 2), (1, 8))),
        "precond": gaussian(own_keys[5], (QUERIES, OUT, IN), (OUT * IN) ** -0.5, 0.0007324219, ((2, 16),)),
    }


def reference(token_index, act_pool, grad_pool, basis_in, basis_out, precond):
    shard_start = (jnp.arange(N_FEAT, dtype=jnp.int32) * TOK_SHARD)[:, None]
    rows = (shard_start + token_index).reshape(-1).astype(jnp.int32)
    act = act_pool[rows]
    grads = grad_pool[rows]
    act_rot = jnp.dot(act, basis_in, preferred_element_type=jnp.float32).astype(jnp.bfloat16)
    grad_rot = jnp.dot(grads, basis_out, preferred_element_type=jnp.float32).astype(jnp.bfloat16)
    grad_wide = grad_rot.astype(jnp.float32)

    def one_query(matrix):
        inner = jnp.dot(act_rot, matrix.T, preferred_element_type=jnp.float32)
        return jnp.sum(grad_wide * inner, axis=1)

    scores = lax.map(one_query, precond)
    return scores, act_rot, grad_rot
```

```python
import functools

import jax
import jax.numpy as jnp
from jax import lax
from jax.experimental import pallas as pl
from jax.experimental.pallas import tpu as pltpu
from jax.sharding import PartitionSpec as P

BF16 = jnp.bfloat16
F32 = jnp.float32
VMEM = pl.BlockSpec(memory_space=pltpu.VMEM)
LIMIT = 56 * 2**20


def call(kernel, outs, *args, scratch=(), flops=0, read=0):
    return pl.pallas_call(
        kernel,
        in_specs=[VMEM] * len(args),
        out_specs=[VMEM] * len(outs),
        out_shape=[jax.ShapeDtypeStruct(*o) for o in outs],
        scratch_shapes=list(scratch),
        compiler_params=pltpu.CompilerParams(vmem_limit_bytes=LIMIT),
        cost_estimate=pl.CostEstimate(flops=flops, bytes_accessed=read, transcendentals=0),
    )(*args)


def swap(x, axis, step):
    n = lax.axis_size(axis)
    return lax.ppermute(x, axis, [(i, i ^ step) for i in range(n)])


def select_kernel(order_ref, act_ref, grad_ref, act_out, grad_out):
    n = act_ref.shape[0]
    hot = (order_ref[...] == lax.broadcasted_iota(jnp.int32, (n, n), 1)).astype(BF16)
    act_out[...] = jnp.dot(hot, act_ref[...], preferred_element_type=F32).astype(BF16)
    grad_out[...] = jnp.dot(hot, grad_ref[...], preferred_element_type=F32).astype(BF16)


def halves(total, keep, give):
    half = total.shape[1] // 2
    low, high = total[:, :half], total[:, half:]
    first = lax.axis_index("tok") == 0
    keep[...] = jnp.where(first, low, high)
    give[...] = jnp.where(first, high, low)


def rotate_kernel(depth, *refs):
    *shards, basis, keep, give, rows, total = refs
    me = lax.axis_index("feat")
    n = shards[0].shape[0]
    for step, shard in enumerate(shards):
        rows[pl.ds(pl.multiple_of((me ^ step) * n, n), n), :] = shard[...]
    total[...] = jnp.zeros_like(total)

    def body(i, carry):
        at = pl.ds(pl.multiple_of(i * depth, depth), depth)
        total[...] += jnp.dot(rows[:, at], basis[at, :], preferred_element_type=F32)
        return carry

    lax.fori_loop(0, basis.shape[0] // depth, body, 0)
    halves(total, keep, give)


def rotate(shards, basis, depth):
    n, k = shards[0].shape
    tokens, width = n * len(shards), basis.shape[1]
    half = ((tokens, width // 2), F32)
    return call(
        functools.partial(rotate_kernel, depth), [half, half], *shards, basis,
        scratch=[pltpu.VMEM((tokens, k), BF16), pltpu.VMEM((tokens, width), F32)],
        flops=2 * tokens * k * width, read=k * width * 2,
    )


def add_kernel(a_ref, b_ref, out):
    out[...] = (a_ref[...] + b_ref[...]).astype(BF16)


def query_kernel(*refs):
    *blocks, precond, out = refs
    me, tok = lax.axis_index("feat"), lax.axis_index("tok")
    n = len(blocks) // 2
    w = blocks[0].shape[1]
    for q in range(precond.shape[0]):
        total = None
        for i, block in enumerate(blocks):
            owner = ((me ^ (i % n)) * 2 + (tok ^ (i // n))) * w
            part = precond[q, pl.ds(pl.multiple_of(owner, w), w), :]
            term = jnp.dot(block[...], part, preferred_element_type=F32)
            total = term if total is None else total + term
        out[q] = total


def score_kernel(mine, theirs, wide, act_rot, out):
    rot = (mine[...] + theirs[...]).astype(BF16)
    act_rot[...] = rot
    rot = rot.astype(F32)
    value = jnp.sum(wide[...] * rot[None], axis=2)
    for i in range(out.shape[0]):
        out[i] = value


def gather(x):
    n = lax.axis_size("feat")
    got = {0: x}
    far = sorted(range(2, n, 2), reverse=True)
    for step in far:
        got[step] = swap(x, "feat", step)
    got[1] = swap(x, "feat", 1)
    for step in far:
        got[step ^ 1] = swap(got[step], "feat", 1)
    return [got[i] for i in range(n)]


def shards(token_index, act_pool, grad_pool, basis_in, basis_out, precond):
    n = lax.axis_size("feat")
    stored, act_width = act_pool.shape
    tokens = stored * n
    act, grads = call(
        select_kernel, [(act_pool.shape, BF16), (grad_pool.shape, BF16)],
        token_index.reshape(-1, 1), act_pool, grad_pool,
    )
    grad_all = gather(grads)
    act_all = gather(act)
    keep, give = rotate(grad_all, basis_out, basis_out.shape[0] // 2)
    (grad_rot,) = call(add_kernel, [(keep.shape, BF16)], keep, swap(give, "tok", 1))
    blocks = gather(grad_rot)
    blocks += [swap(b, "tok", 1) for b in blocks]
    queries, _, width = precond.shape
    (wide,) = call(
        query_kernel, [((queries, tokens, width), F32)], *blocks, precond,
        flops=2 * tokens * precond.size, read=precond.size * 2,
    )
    keep, give = rotate(act_all, basis_in, act_width // 4)
    act_rot, parts = call(
        score_kernel, [(keep.shape, BF16), ((2 * n, queries, tokens), F32)],
        keep, swap(give, "tok", 1), wide,
    )
    scores = lax.all_to_all(parts, ("feat", "tok"), 0, 0, tiled=True).sum(axis=0)
    return scores, act_rot, grad_rot


def solution(mesh):
    placed = (
        P(("parts", "feat"), None),
        P(("parts", "feat"), "tok"),
        P(("parts", "feat"), "tok"),
        P(("parts", "tok"), "feat"),
        P(("parts", "tok"), "feat"),
        P("parts", None, ("feat", "tok")),
    )
    return jax.shard_map(
        shards,
        mesh=mesh,
        in_specs=placed,
        out_specs=(P("parts", None), P("parts", ("feat", "tok")), P("parts", ("feat", "tok"))),
        check_vma=False,
    )
```

```python
import functools
import math

import jax
import jax.numpy as jnp
from jax import lax
from jax.experimental import pallas as pl
from jax.experimental.pallas import tpu as pltpu
from jax.sharding import PartitionSpec as P

BF16 = jnp.bfloat16
F32 = jnp.float32
VMEM = pl.BlockSpec(memory_space=pltpu.VMEM)
ANY = pl.BlockSpec(memory_space=pl.ANY)
ROOM = 4 * 2**20


def call(kernel, outs, *args, scratch=(), flops=0, read=0, specs=None):
    held = [(s.shape, s.dtype) for s in scratch if hasattr(s, "inner_aval")] + list(outs)
    held = sum(math.prod(shape) * jnp.dtype(dtype).itemsize for shape, dtype in held)
    return pl.pallas_call(
        kernel,
        in_specs=specs or [VMEM] * len(args),
        out_specs=[VMEM] * len(outs),
        out_shape=[jax.ShapeDtypeStruct(*o) for o in outs],
        scratch_shapes=list(scratch),
        compiler_params=pltpu.CompilerParams(vmem_limit_bytes=ROOM + held),
        cost_estimate=pl.CostEstimate(flops=flops, bytes_accessed=read, transcendentals=0),
    )(*args)


def swap(x, axis, step):
    n = lax.axis_size(axis)
    return lax.ppermute(x, axis, [(i, i ^ step) for i in range(n)])


def pick(order_ref, pool):
    n = pool.shape[0]
    hot = (order_ref[...] == lax.broadcasted_iota(jnp.int32, (n, n), 0)).astype(BF16)
    rows = lax.dot_general(hot, pool[...], (((0,), (0,)), ((), ())), preferred_element_type=F32)
    return rows.astype(BF16)


def select_kernel(order_ref, pool, out, order_in, pool_in, order_sem, pool_sem):
    first = pltpu.make_async_copy(order_ref, order_in, order_sem)
    second = pltpu.make_async_copy(pool, pool_in, pool_sem)
    first.start()
    second.start()
    first.wait()
    second.wait()
    out[...] = pick(order_in, pool_in)


def select_bundle_kernel(order_ref, pool, *refs):
    *near, out, bundle = refs
    for i, shard in enumerate(near):
        bundle[i] = shard[...]
    out[...] = pick(order_ref, pool)


def halves(total, keep, give):
    half = total.shape[1] // 2
    low, high = total[:, :half], total[:, half:]
    first = lax.axis_index("tok") == 0
    keep[...] = jnp.where(first, low, high)
    give[...] = jnp.where(first, high, low)


def bundle_kernel(count, *refs):
    out = refs[-1]
    for i in range(count):
        out[i] = refs[i][...]


def bundle(xs, deps=()):
    (out,) = call(
        functools.partial(bundle_kernel, len(xs)), [((len(xs),) + xs[0].shape, xs[0].dtype)],
        *xs, *deps, specs=[VMEM] * len(xs) + [ANY] * len(deps),
    )
    return out


def rotate_kernel(depth, near, far, *refs):
    near, refs = refs[:near], refs[near:]
    far, (basis, keep, give, rows, total) = refs[:far], refs[far:]
    me = lax.axis_index("feat")
    n = near[0].shape[0]
    far = [one.at[i] for one in far for i in range(one.shape[0])]
    for i, (mine, other) in enumerate(zip(near, far)):
        rows[pl.ds(pl.multiple_of((me ^ (2 * i)) * n, n), n), :] = mine[...]
        rows[pl.ds(pl.multiple_of((me ^ (2 * i + 1)) * n, n), n), :] = other[...]
    total[...] = jnp.zeros_like(total)

    def body(i, carry):
        at = pl.ds(pl.multiple_of(i * depth, depth), depth)
        total[...] += jnp.dot(rows[:, at], basis[at, :], preferred_element_type=F32)
        return carry

    lax.fori_loop(0, basis.shape[0] // depth, body, 0)
    halves(total, keep, give)


def rotate(near, far, basis, depth, flops):
    n, k = near[0].shape
    tokens, width = 2 * n * len(near), basis.shape[1]
    half = ((tokens, width // 2), F32)
    return call(
        functools.partial(rotate_kernel, depth, len(near), len(far)), [half, half], *near, *far, basis,
        scratch=[pltpu.VMEM((tokens, k), BF16), pltpu.VMEM((tokens, width), F32)],
        flops=flops, read=k * width * 2,
    )


def add_kernel(a_ref, b_ref, out, again):
    total = (a_ref[...] + b_ref[...]).astype(BF16)
    out[...] = total
    again[...] = total


def query_kernel(*refs):
    *blocks, precond, out = refs
    me, tok = lax.axis_index("feat"), lax.axis_index("tok")
    count, _, w = blocks[0].shape
    for q in range(precond.shape[0]):
        total = None
        for i, block in enumerate(blocks):
            for j in range(count):
                owner = ((me ^ (2 * j + i % 2)) * 2 + (tok ^ (i // 2))) * w
                part = precond[q, pl.ds(pl.multiple_of(owner, w), w), :]
                term = jnp.dot(block[j], part, preferred_element_type=F32)
                total = term if total is None else total + term
        out[q] = total


def score_kernel(mine, theirs, wide, act_rot, out):
    rot = (mine[...] + theirs[...]).astype(BF16)
    act_rot[...] = rot
    rot = rot.astype(F32)
    value = jnp.sum(wide[...] * rot[None], axis=2)
    for i in range(out.shape[0]):
        out[i] = value


def across(x):
    return [x] + [swap(x, "feat", step) for step in range(2, lax.axis_size("feat"), 2)]


def after(x, *deps):
    return lax.optimization_barrier((x,) + deps)[0]


def shards(token_index, act_pool, grad_pool, basis_in, basis_out, precond):
    n = lax.axis_size("feat")
    stored, act_width = act_pool.shape
    tokens = stored * n
    (grads,) = call(
        select_kernel, [(grad_pool.shape, BF16)], token_index, grad_pool,
        specs=[ANY, ANY], flops=4000 * basis_out.size,
        scratch=[
            pltpu.VMEM(token_index.shape, jnp.int32), pltpu.VMEM(grad_pool.shape, BF16),
            pltpu.SemaphoreType.DMA, pltpu.SemaphoreType.DMA,
        ],
    )
    near = across(grads)
    act, near_bundle = call(
        select_bundle_kernel, [(act_pool.shape, BF16), ((n // 2,) + grads.shape, BF16)],
        token_index, act_pool, *near, flops=800 * basis_in.size,
    )
    act_near = across(act)
    keep, give = rotate(near, [swap(near_bundle, "feat", 1)], basis_out, basis_out.shape[0] // 2, 800 * precond.size)
    half = len(act_near) // 2
    act_far = [swap(bundle(act_near[:half]), "feat", 1)]
    grad_rot, block = call(add_kernel, [(keep.shape, BF16)] * 2, keep, swap(give, "tok", 1))
    act_far += [swap(bundle(act_near[half:], [block]), "feat", 1)]
    mine = bundle(across(block))
    other = swap(mine, "feat", 1)
    blocks = [mine, other, swap(mine, "tok", 1), swap(other, "tok", 1)]
    queries, _, width = precond.shape
    (wide,) = call(
        query_kernel, [((queries, tokens, width), F32)], *blocks, precond,
        flops=2 * tokens * precond.size, read=precond.size * 2,
    )
    act_near[0] = after(act_near[0], mine)
    keep, give = rotate(act_near, act_far, basis_in, act_width // 4, 1600 * precond.size)
    act_rot, parts = call(
        score_kernel, [(keep.shape, BF16), ((2 * n, queries, tokens), F32)],
        keep, swap(give, "tok", 1), wide,
    )
    scores = lax.all_to_all(parts, ("feat", "tok"), 0, 0, tiled=True).sum(axis=0)
    return scores, act_rot, grad_rot


def solution(mesh):
    placed = (
        P(("parts", "feat"), None),
        P(("parts", "feat"), "tok"),
        P(("parts", "feat"), "tok"),
        P(("parts", "tok"), "feat"),
        P(("parts", "tok"), "feat"),
        P("parts", None, ("feat", "tok")),
    )
    return jax.shard_map(
        shards,
        mesh=mesh,
        in_specs=placed,
        out_specs=(P("parts", None), P("parts", ("feat", "tok")), P("parts", ("feat", "tok"))),
        check_vma=False,
    )
```

```python
import functools
import math

import jax
import jax.numpy as jnp
from jax import lax
from jax.experimental import pallas as pl
from jax.experimental.pallas import tpu as pltpu
from jax.sharding import PartitionSpec as P

BF16 = jnp.bfloat16
F32 = jnp.float32
VMEM = pl.BlockSpec(memory_space=pltpu.VMEM)
ANY = pl.BlockSpec(memory_space=pl.ANY)
ROOM = 4 * 2**20


def call(kernel, outs, *args, scratch=(), flops=0, read=0, specs=None, room=ROOM):
    held = [(s.shape, s.dtype) for s in scratch if getattr(s, "memory_space", None) == pltpu.VMEM] + list(outs)
    held = sum(math.prod(shape) * jnp.dtype(dtype).itemsize for shape, dtype in held)
    return pl.pallas_call(
        kernel,
        in_specs=specs or [VMEM] * len(args),
        out_specs=[VMEM] * len(outs),
        out_shape=[jax.ShapeDtypeStruct(*o) for o in outs],
        scratch_shapes=list(scratch),
        compiler_params=pltpu.CompilerParams(vmem_limit_bytes=room + held),
        cost_estimate=pl.CostEstimate(flops=flops, bytes_accessed=read, transcendentals=0),
    )(*args)


def swap(x, axis, step):
    n = lax.axis_size(axis)
    return lax.ppermute(x, axis, [(i, i ^ step) for i in range(n)])


def pick(order_ref, pool):
    n = pool.shape[0]
    hot = (order_ref[...] == lax.broadcasted_iota(jnp.int32, (n, n), 0)).astype(BF16)
    rows = lax.dot_general(hot, pool[...], (((0,), (0,)), ((), ())), preferred_element_type=F32)
    return rows.astype(BF16)


def select(token_index, pool, deps=(), flops=0):
    hot = (token_index[0][:, None] == jnp.arange(pool.shape[0])[None]).astype(BF16)
    if deps:
        hot = after(hot, *deps)
    return jnp.dot(hot, pool, preferred_element_type=F32).astype(BF16)


def halves(total, keep, give):
    half = total.shape[1] // 2
    low, high = total[:, :half], total[:, half:]
    first = lax.axis_index("tok") == 0
    keep[...] = jnp.where(first, low, high)
    give[...] = jnp.where(first, high, low)


def bundle_kernel(count, *refs):
    out = refs[-1]
    for i in range(count):
        out[i] = refs[i][...]


def bundle(xs, deps=(), flops=0):
    (out,) = call(
        functools.partial(bundle_kernel, len(xs)), [((len(xs),) + xs[0].shape, xs[0].dtype)],
        *xs, *deps, specs=[VMEM] * len(xs) + [ANY] * len(deps), flops=flops,
    )
    return out


def is_inner(me):
    z = me // 2
    return ((z ^ (z // 2)) & 1) == 1


def choose_kernel(inner_ref, end_ref, out):
    out[...] = jnp.where(is_inner(lax.axis_index("feat")), inner_ref[...], end_ref[...])


def choose(inner, end):
    return call(choose_kernel, [(inner.shape, inner.dtype)], inner, end)[0]


def pair_middle(x):
    to = [i ^ 6 if i // 2 in (1, 2) else i ^ 1 for i in range(8)]
    return lax.ppermute(x, "feat", list(enumerate(to)))


def relay_place(me):
    z, y = me // 2, me % 2
    inner = is_inner(me)
    mid = jnp.where(inner, z ^ 3, z ^ 2)
    near, other = z ^ 1, y ^ 1
    out = mid ^ 1
    return [
        z * 2 + y,
        near * 2 + y,
        jnp.where(inner, mid * 2 + y, z * 2 + other),
        jnp.where(inner, out * 2 + y, near * 2 + other),
        jnp.where(inner, near * 2 + other, mid * 2 + y),
        jnp.where(inner, z * 2 + other, out * 2 + y),
        mid * 2 + other,
        out * 2 + other,
    ]


def direct_place(me, m):
    return [me ^ (2 * i + side) for side in range(2) for i in range(m)]


def rows_of(refs):
    return [ref.at[i] for ref in refs for i in range(ref.shape[0])]


def rotate_kernel(depth, place, *refs):
    shards = rows_of(refs[:-5])
    basis, keep, give, rows, total = refs[-5:]
    n = shards[0].shape[0]
    for owner, shard in zip(place(lax.axis_index("feat")), shards):
        rows[pl.ds(pl.multiple_of(owner * n, n), n), :] = shard[...]
    total[...] = jnp.zeros_like(total)

    def body(i, carry):
        at = pl.ds(pl.multiple_of(i * depth, depth), depth)
        total[...] += jnp.dot(rows[:, at], basis[at, :], preferred_element_type=F32)
        return carry

    lax.fori_loop(0, basis.shape[0] // depth, body, 0)
    halves(total, keep, give)


def rotate(shards, place, basis, depth, flops):
    _, n, k = shards[0].shape
    tokens, width = n * lax.axis_size("feat"), basis.shape[1]
    half = ((tokens, width // 2), F32)
    return call(
        functools.partial(rotate_kernel, depth, place), [half, half], *shards, basis,
        scratch=[pltpu.VMEM((tokens, k), BF16), pltpu.VMEM((tokens, width), F32)],
        flops=flops, read=k * width * 2,
    )


def add_kernel(a_ref, b_ref, out, again):
    total = (a_ref[...] + b_ref[...]).astype(BF16)
    out[...] = total
    again[...] = total


def query_kernel(side, mine, theirs, precond, *refs):
    *so_far, out = refs
    me, tok = lax.axis_index("feat"), lax.axis_index("tok")
    count, _, w = mine.shape
    for q in range(precond.shape[0]):
        total = so_far[0][q] if so_far else None
        for i, block in enumerate((mine, theirs)):
            for j in range(count):
                owner = ((me ^ (2 * j + side)) * 2 + (tok ^ i)) * w
                part = precond[q, pl.ds(pl.multiple_of(owner, w), w), :]
                term = jnp.dot(block[j], part, preferred_element_type=F32)
                total = term if total is None else total + term
        out[q] = total


def query(side, mine, theirs, precond, so_far):
    queries, _, width = precond.shape
    tokens = mine.shape[1]
    (out,) = call(
        functools.partial(query_kernel, side), [((queries, tokens, width), F32)],
        mine, theirs, precond, *so_far,
        flops=tokens * precond.size, read=precond.size,
    )
    return out


def score_kernel(mine, theirs, wide, act_rot, out):
    rot = (mine[...] + theirs[...]).astype(BF16)
    act_rot[...] = rot
    rot = rot.astype(F32)
    value = jnp.sum(wide[...] * rot[None], axis=2)
    for i in range(out.shape[0]):
        out[i] = value


def across(x):
    return [x] + [swap(x, "feat", step) for step in range(2, lax.axis_size("feat"), 2)]


def after(x, *deps):
    return lax.optimization_barrier((x,) + deps)[0]


def shards(token_index, act_pool, grad_pool, basis_in, basis_out, precond):
    n = lax.axis_size("feat")
    stored, act_width = act_pool.shape
    tokens, queries = stored * n, precond.shape[0]
    m = n // 2
    relay = n == 8
    direct = functools.partial(direct_place, m=m)
    grads = select(token_index, grad_pool, flops=4000 * basis_out.size)
    near = across(grads)
    act = select(token_index, act_pool, near[1:2])
    first = [swap(act, "feat", 2), pair_middle(act)] if relay else [swap(act, "feat", 1)]
    near_bundle = bundle(near, [act], 800 * basis_in.size)
    far_bundle = after(swap(near_bundle, "feat", 1), *first)
    if relay:
        z1, m1 = first
        m2, o2 = pair_middle(z1), swap(m1, "feat", 2)
    else:
        act_near = across(after(act, near_bundle))
    keep, give = rotate(
        [near_bundle, far_bundle], direct, basis_out, basis_out.shape[0] // 2, 256 * basis_out.size,
    )
    grad_rot, block = call(
        add_kernel, [(keep.shape, BF16)] * 2, keep, swap(give, "tok", 1),
    )
    if relay:
        o3, y2 = swap(after(m2, block), "feat", 2), swap(choose(after(m1, block), o2), "feat", 1)
        mine = bundle(across(block), [o3, y2])
        y3 = swap(choose(m2, o3), "feat", 1)
        act_all, place = [act, z1, m1, m2, o2, o3, y2, y3], relay_place
    else:
        act_far = swap(bundle(act_near[1:], [block]), "feat", 1)
        mine = bundle(across(block))
        act_all, place = act_near + first + [act_far], direct
    wide = query(0, mine, swap(mine, "tok", 1), precond, [])
    other = swap(mine, "feat", 1)
    act_all[0] = after(act_all[0], wide)
    wide = query(1, other, swap(other, "tok", 1), precond, [wide])
    act_all = [x if x.ndim == 3 else x[None] for x in act_all]
    keep, give = rotate(act_all, place, basis_in, act_width // 4, 1600 * precond.size)
    act_rot, parts = call(
        score_kernel, [(keep.shape, BF16), ((2 * n, queries, tokens), F32)],
        keep, swap(give, "tok", 1), wide,
    )
    scores = lax.all_to_all(parts, ("feat", "tok"), 0, 0, tiled=True).sum(axis=0)
    return scores, act_rot, grad_rot


def solution(mesh):
    placed = (
        P(("parts", "feat"), None),
        P(("parts", "feat"), "tok"),
        P(("parts", "feat"), "tok"),
        P(("parts", "tok"), "feat"),
        P(("parts", "tok"), "feat"),
        P("parts", None, ("feat", "tok")),
    )
    return jax.shard_map(
        shards,
        mesh=mesh,
        in_specs=placed,
        out_specs=(P("parts", None), P("parts", ("feat", "tok")), P("parts", ("feat", "tok"))),
        check_vma=False,
    )
```

```python
import functools
import math

import jax
import jax.numpy as jnp
from jax import lax
from jax.experimental import pallas as pl
from jax.experimental.pallas import tpu as pltpu
from jax.sharding import PartitionSpec as P

BF16 = jnp.bfloat16
F32 = jnp.float32
VMEM = pl.BlockSpec(memory_space=pltpu.VMEM)
ANY = pl.BlockSpec(memory_space=pl.ANY)
ROOM = 4 * 2**20


def call(kernel, outs, *args, scratch=(), flops=0, read=0, specs=None, room=ROOM):
    held = [(s.shape, s.dtype) for s in scratch if getattr(s, "memory_space", None) == pltpu.VMEM] + list(outs)
    held = sum(math.prod(shape) * jnp.dtype(dtype).itemsize for shape, dtype in held)
    return pl.pallas_call(
        kernel,
        in_specs=specs or [VMEM] * len(args),
        out_specs=[VMEM] * len(outs),
        out_shape=[jax.ShapeDtypeStruct(*o) for o in outs],
        scratch_shapes=list(scratch),
        compiler_params=pltpu.CompilerParams(vmem_limit_bytes=room + held),
        cost_estimate=pl.CostEstimate(flops=flops, bytes_accessed=read, transcendentals=0),
    )(*args)


def swap(x, axis, step):
    n = lax.axis_size(axis)
    return lax.ppermute(x, axis, [(i, i ^ step) for i in range(n)])


def pick(order_ref, pool):
    n = pool.shape[0]
    hot = (order_ref[...] == lax.broadcasted_iota(jnp.int32, (n, n), 0)).astype(BF16)
    rows = lax.dot_general(hot, pool[...], (((0,), (0,)), ((), ())), preferred_element_type=F32)
    return rows.astype(BF16)


def select(token_index, pool, deps=(), flops=0):
    hot = (token_index[0][:, None] == jnp.arange(pool.shape[0])[None]).astype(BF16)
    if deps:
        hot = after(hot, *deps)
    return jnp.dot(hot, pool, preferred_element_type=F32).astype(BF16)


def halves(total, keep, give):
    half = total.shape[1] // 2
    low, high = total[:, :half], total[:, half:]
    first = lax.axis_index("tok") == 0
    keep[...] = jnp.where(first, low, high)
    give[...] = jnp.where(first, high, low)


def bundle_kernel(count, *refs):
    out = refs[-1]
    for i in range(count):
        out[i] = refs[i][...]


def bundle(xs, deps=(), flops=0):
    (out,) = call(
        functools.partial(bundle_kernel, len(xs)), [((len(xs),) + xs[0].shape, xs[0].dtype)],
        *xs, *deps, specs=[VMEM] * len(xs) + [ANY] * len(deps), flops=flops,
    )
    return out


def is_inner(me):
    z = me // 2
    return ((z ^ (z // 2)) & 1) == 1


def choose_kernel(inner_ref, end_ref, out):
    out[...] = jnp.where(is_inner(lax.axis_index("feat")), inner_ref[...], end_ref[...])


def choose(inner, end):
    return call(choose_kernel, [(inner.shape, inner.dtype)], inner, end)[0]


def pair_middle(x):
    to = [i ^ 6 if i // 2 in (1, 2) else i ^ 1 for i in range(8)]
    return lax.ppermute(x, "feat", list(enumerate(to)))


def relay_place(me):
    z, y = me // 2, me % 2
    inner = is_inner(me)
    mid = jnp.where(inner, z ^ 3, z ^ 2)
    near, other = z ^ 1, y ^ 1
    out = mid ^ 1
    return [
        z * 2 + y,
        near * 2 + y,
        jnp.where(inner, mid * 2 + y, z * 2 + other),
        jnp.where(inner, out * 2 + y, near * 2 + other),
        jnp.where(inner, near * 2 + other, mid * 2 + y),
        jnp.where(inner, z * 2 + other, out * 2 + y),
        mid * 2 + other,
        out * 2 + other,
    ]


def direct_place(me, m):
    return [me ^ (2 * i + side) for side in range(2) for i in range(m)]


def rows_of(refs):
    return [ref.at[i] for ref in refs for i in range(ref.shape[0])]


def rotate_kernel(depth, place, *refs):
    shards = rows_of(refs[:-5])
    basis, keep, give, rows, total = refs[-5:]
    n = shards[0].shape[0]
    for owner, shard in zip(place(lax.axis_index("feat")), shards):
        rows[pl.ds(pl.multiple_of(owner * n, n), n), :] = shard[...]
    total[...] = jnp.zeros_like(total)

    def body(i, carry):
        at = pl.ds(pl.multiple_of(i * depth, depth), depth)
        total[...] += jnp.dot(rows[:, at], basis[at, :], preferred_element_type=F32)
        return carry

    lax.fori_loop(0, basis.shape[0] // depth, body, 0)
    halves(total, keep, give)


def rotate(shards, place, basis, depth, flops):
    _, n, k = shards[0].shape
    tokens, width = n * lax.axis_size("feat"), basis.shape[1]
    half = ((tokens, width // 2), F32)
    return call(
        functools.partial(rotate_kernel, depth, place), [half, half], *shards, basis,
        scratch=[pltpu.VMEM((tokens, k), BF16), pltpu.VMEM((tokens, width), F32)],
        flops=flops, read=k * width * 2,
    )


def add_kernel(a_ref, b_ref, out, again):
    total = (a_ref[...] + b_ref[...]).astype(BF16)
    out[...] = total
    again[...] = total


def terms(side, flips, blocks, precond, q, total):
    me, tok = lax.axis_index("feat"), lax.axis_index("tok")
    for flip, block in zip(flips, blocks):
        count, _, w = block.shape
        for j in range(count):
            owner = ((me ^ (2 * j + side)) * 2 + (tok ^ flip)) * w
            part = precond[q, pl.ds(pl.multiple_of(owner, w), w), :]
            term = jnp.dot(block[j], part, preferred_element_type=F32)
            total = term if total is None else total + term
    return total


def query_kernel(side, flips, *refs):
    blocks, (precond, *so_far, out) = refs[:len(flips)], refs[len(flips):]
    for q in range(precond.shape[0]):
        out[q] = terms(side, flips, blocks, precond, q, so_far[0][q] if so_far else None)


def query(side, blocks, precond, so_far=()):
    queries, _, width = precond.shape
    tokens = next(iter(blocks.values())).shape[1]
    (out,) = call(
        functools.partial(query_kernel, side, tuple(blocks)), [((queries, tokens, width), F32)],
        *blocks.values(), precond, *so_far,
        flops=len(blocks) * tokens * precond.size // 2, read=len(blocks) * precond.size // 2,
    )
    return out


def score_kernel(mine, theirs, block, precond, wide, act_rot, out):
    rot = (mine[...] + theirs[...]).astype(BF16)
    act_rot[...] = rot
    rot = rot.astype(F32)
    for q in range(precond.shape[0]):
        value = jnp.sum(terms(1, (1,), (block,), precond, q, wide[q]) * rot, axis=1)
        for i in range(out.shape[0]):
            out[i, q] = value


def across(x):
    return [x] + [swap(x, "feat", step) for step in range(2, lax.axis_size("feat"), 2)]


def after(x, *deps):
    return lax.optimization_barrier((x,) + deps)[0]


def shards(token_index, act_pool, grad_pool, basis_in, basis_out, precond):
    n = lax.axis_size("feat")
    stored, act_width = act_pool.shape
    tokens, queries = stored * n, precond.shape[0]
    m = n // 2
    relay = n == 8
    direct = functools.partial(direct_place, m=m)
    grads = select(token_index, grad_pool, flops=4000 * basis_out.size)
    near = across(grads)
    act = select(token_index, act_pool, near[1:2])
    first = [swap(act, "feat", 2), pair_middle(act)] if relay else [swap(act, "feat", 1)]
    near_bundle = bundle(near, [act], 800 * basis_in.size)
    far_bundle = after(swap(near_bundle, "feat", 1), *first)
    if relay:
        z1, m1 = first
        m2, o2 = pair_middle(z1), swap(m1, "feat", 2)
    else:
        act_near = across(after(act, near_bundle))
    keep, give = rotate(
        [near_bundle, far_bundle], direct, basis_out, basis_out.shape[0] // 2, 256 * basis_out.size,
    )
    grad_rot, block = call(
        add_kernel, [(keep.shape, BF16)] * 2, keep, swap(give, "tok", 1),
    )
    if relay:
        o3, y2 = swap(after(m2, block), "feat", 2), swap(choose(after(m1, block), o2), "feat", 1)
        mine = bundle(across(block), [o3, y2])
        y3 = swap(choose(m2, o3), "feat", 1)
        act_all, place = [act, z1, m1, m2, o2, o3, y2, y3], relay_place
    else:
        act_far = swap(bundle(act_near[1:], [block]), "feat", 1)
        mine = bundle(across(block))
        act_all, place = act_near + first + [act_far], direct
    wide = query(0, {0: mine, 1: swap(mine, "tok", 1)}, precond)
    other = swap(mine, "feat", 1)
    act_all[0] = after(act_all[0], wide)
    wide = query(1, {0: other}, precond, [wide])
    act_all = [x if x.ndim == 3 else x[None] for x in act_all]
    keep, give = rotate(act_all, place, basis_in, act_width // 4, 1600 * precond.size)
    act_rot, parts = call(
        score_kernel, [(keep.shape, BF16), ((2 * n, queries, tokens), F32)],
        keep, swap(give, "tok", 1), swap(other, "tok", 1), precond, wide,
    )
    scores = lax.all_to_all(parts, ("feat", "tok"), 0, 0, tiled=True).sum(axis=0)
    return scores, act_rot, grad_rot


def solution(mesh):
    placed = (
        P(("parts", "feat"), None),
        P(("parts", "feat"), "tok"),
        P(("parts", "feat"), "tok"),
        P(("parts", "tok"), "feat"),
        P(("parts", "tok"), "feat"),
        P("parts", None, ("feat", "tok")),
    )
    return jax.shard_map(
        shards,
        mesh=mesh,
        in_specs=placed,
        out_specs=(P("parts", None), P("parts", ("feat", "tok")), P("parts", ("feat", "tok"))),
        check_vma=False,
    )
```
